256 devices in a mesh: node: 32 (over y, z), col: 8 (over x, core).
Axes of the slice: x: 4, y: 4, z: 8, core: 2. Of those that a mesh axis runs over, the one named last changes fastest.
Arguments:
- tile_values: bfloat16 [12288, 128, 128], P('node'), as said below
- tile_rows: int32 [12288], P('node'), may hold values from 0 to 3, as said below
- tile_cols: int32 [12288], P('node'), may hold values from 0 to 127, as said below
- tile_live: int32 [32], P('node'), may hold values from 192 to 384
- degrees: int32 [16384], P('node'), may hold values from 0 to 4095
- projection: int32 [16384, 512], P('node', 'col'), may hold values from -1 to 1
- term_weights: float32 [4], replicated, may hold values from 0.25 to 1.5
Outputs:
- embedding: float32 [16384, 512], P('node', 'col')
The draws below stay inside these ranges and needn't reach their ends.
Inputs may be any that keep to these rules, and one draw needn't show every extreme that they name: `tile_rows`: local row block of the slot. `tile_cols`: the live slots of one device read exactly one column block from the row blocks of each device; every such device-to-device pair reads at least one. `tile_values`: weights are non-negative; some nodes have no edges.
All inputs are finite; a program needn't handle non-finite values.
Results may differ from the reference program's by a relative error of at most 0.0029.
Values may be sent and summed in bfloat16 or wider, within the bound.
A program may use at most 128 MiB of HBM per device.

```python
import math
import jax
import jax.numpy as jnp
import numpy as np
from jax import lax

DIM = 512
TILE = 128
TERMS = 4
SLOT = 1
TILE_PER_BLK = 96
BLK_DEV = 4
TILES_DEV = 384
NODES = 16384
N_NODE = 32


def tile_pattern(key):
    key = jax.random.fold_in(key, 101)
    keys = jax.random.split(key, 8)
    pairs = jax.random.randint(keys[0], (N_NODE, N_NODE), 1, SLOT + 1)
    fullest = jax.random.randint(keys[1], (N_NODE,), 0, N_NODE)
    pairs = jnp.where(jnp.arange(N_NODE)[None, :] == fullest[:, None], SLOT, pairs)
    perm_keys = jax.random.split(keys[2], N_NODE * N_NODE)
    orders = jax.vmap(lambda one_key: jax.random.permutation(one_key, BLK_DEV))(perm_keys)
    orders = orders.reshape(N_NODE, N_NODE, BLK_DEV)
    lowest = jnp.arange(BLK_DEV)[None, None, :]
    highest = BLK_DEV - 1 - jnp.arange(BLK_DEV)[None, None, :]
    reader_zero = jnp.arange(N_NODE)[:, None, None] == 0
    owner_first = jnp.arange(N_NODE)[None, :, None] == 0
    owner_last = jnp.arange(N_NODE)[None, :, None] == N_NODE - 1
    orders = jnp.where(reader_zero & owner_first, lowest, orders)
    orders = jnp.where(reader_zero & owner_last, highest, orders)
    orders = orders[:, :, :SLOT]
    candidates = (jnp.arange(N_NODE)[None, :, None] * BLK_DEV + orders).reshape(N_NODE, N_NODE * SLOT)
    valid = (jnp.arange(SLOT)[None, None, :] < pairs[:, :, None]).reshape(N_NODE, N_NODE * SLOT)
    placing = jnp.argsort(jnp.where(valid, 0, 1), axis=1, stable=True)
    compact = jnp.take_along_axis(candidates, placing, axis=1)
    valid_count = jnp.sum(valid.astype(jnp.int32), axis=1)
    picks = jax.random.randint(keys[3], (N_NODE, TILES_DEV), 0, 1 << 20)
    slots = jnp.arange(TILES_DEV)[None, :]
    where_col = jnp.where(slots < valid_count[:, None], slots, picks % valid_count[:, None])
    cols = jnp.take_along_axis(compact, where_col, axis=1)
    live = jax.random.randint(keys[4], (N_NODE,), TILES_DEV // 2, TILES_DEV + 1)
    busiest = jax.random.randint(keys[5], (), 0, N_NODE)
    live = jnp.where(jnp.arange(N_NODE) == busiest, TILES_DEV, live)
    rows = jax.random.randint(keys[6], (N_NODE, TILES_DEV), 0, BLK_DEV)
    dangling = jax.random.randint(keys[7], (N_NODE, BLK_DEV, TILE), 0, 16) == 0
    return (rows, cols, live, dangling)


def draw_tile_rows(key, part):
    rows, cols, live, dangling = tile_pattern(key)
    return rows.reshape(N_NODE * TILES_DEV).astype(jnp.int32)


def draw_tile_cols(key, part):
    rows, cols, live, dangling = tile_pattern(key)
    return cols.reshape(N_NODE * TILES_DEV).astype(jnp.int32)


def draw_tile_live(key, part):
    rows, cols, live, dangling = tile_pattern(key)
    return live.astype(jnp.int32)


def draw_tile_values(key, part):
    rows, cols, live, dangling = tile_pattern(key)
    key = jax.random.fold_in(key, 4)
    density_key, mask_key, value_key = jax.random.split(key, 3)
    sparsest = max(0.001, 2.0 / (TILE_PER_BLK * TILE))
    log_density = jax.random.uniform(density_key, (N_NODE, BLK_DEV, TILE), jnp.float32, jnp.log(sparsest), jnp.log(0.4))
    density = jnp.exp(log_density)
    row_density = density[jnp.arange(N_NODE)[:, None], rows]
    present = jax.random.uniform(mask_key, (N_NODE, TILES_DEV, TILE, TILE)) < row_density[:, :, :, None]
    weights = jax.random.uniform(value_key, (N_NODE, TILES_DEV, TILE, TILE), jnp.float32, 0.5, 2.0)
    dead = dangling[jnp.arange(N_NODE)[:, None], rows]
    values = jnp.where(present & ~dead[:, :, :, None], weights, 0.0)
    return values.reshape(N_NODE * TILES_DEV, TILE, TILE).astype(jnp.bfloat16)


def place_ends(result, key, least, largest):
    extent = result.shape
    place = [jax.random.randint(jax.random.fold_in(key, axis), (), 0, extent[axis]) for axis in range(len(extent))]
    result = result.at[tuple(place)].set(least)
    longest = extent.index(max(extent))
    place[longest] = (place[longest] + 1) % extent[longest]
    return result.at[tuple(place)].set(largest)


def cumulative_ranks(amount, lean):
    weights = [(1 << 20) // math.isqrt(standing ** lean) + 1 for standing in range(1, amount + 1)]
    scale = 1 + sum(weights) // (1 << 30)
    return np.cumsum(np.array([max(1, weight // scale) for weight in weights]))


def skewed_ids(rng, extent, count, slope):
    table = cumulative_ranks(count, slope)
    ticket = jax.random.randint(jax.random.fold_in(rng, 1), extent, 0, int(table[count - 1]))
    rank = jnp.searchsorted(jnp.asarray(table, jnp.int32), ticket, side="right")
    return jax.random.permutation(jax.random.fold_in(rng, 2), count)[rank].astype(jnp.int32)


def setup_inputs(seed: int = 0) -> dict:
    seeds = jax.random.split(jax.random.key(seed), 8)
    tile_values = draw_tile_values(jax.random.fold_in(seeds[7], 71), 0)
    tile_rows = draw_tile_rows(jax.random.fold_in(seeds[7], 71), 0)
    tile_cols = draw_tile_cols(jax.random.fold_in(seeds[7], 71), 0)
    tile_live = draw_tile_live(jax.random.fold_in(seeds[7], 71), 0)
    degrees = place_ends(skewed_ids(seeds[4], (NODES,), 4096, 2), jax.random.fold_in(seeds[4], 3), 0, 4095).astype(jnp.int32)
    projection = place_ends(jax.random.randint(seeds[5], (NODES, DIM), -1, 2), jax.random.fold_in(seeds[5], 1), -1, 1).astype(jnp.int32)
    term_weights = jnp.clip(jax.random.uniform(seeds[6], (TERMS,), jnp.float32, 0.25, 1.5), 0.25, 1.5)
    return dict(tile_values=tile_values, tile_rows=tile_rows, tile_cols=tile_cols, tile_live=tile_live, degrees=degrees, projection=projection, term_weights=term_weights)


epsilon = 1e-12

def reference(tile_values, tile_rows, tile_cols, tile_live, degrees, projection, term_weights):
    values = tile_values.reshape(N_NODE, TILES_DEV, TILE, TILE)
    rows = tile_rows.reshape(N_NODE, TILES_DEV)
    cols = tile_cols.reshape(N_NODE, TILES_DEV)
    living = jnp.arange(TILES_DEV)[None, :] < tile_live[:, None]
    owners = ((rows[:, :, None] == jnp.arange(BLK_DEV)[None, None, :]) & living[:, :, None]).astype(jnp.float32)
    row_sums = lax.optimization_barrier(jnp.sum(values, axis=3, dtype=jnp.float32))
    degree_sum = jnp.einsum('dtb,dtr->dbr', owners, row_sums, precision=lax.Precision.HIGHEST)
    inverse = 1.0 / jnp.maximum(degree_sum, 1.0)
    scaling = lax.rsqrt(jnp.maximum(degrees, 1).astype(jnp.float32))
    current = (projection.astype(jnp.float32) * scaling[:, None]).astype(jnp.bfloat16)
    embedding = jnp.zeros((NODES, DIM), jnp.float32)
    for level_index in range(TERMS):
        sources = current.reshape(N_NODE * BLK_DEV, TILE, DIM)

        def device_product(packed):
            device_values, device_cols, device_owners = packed
            picked = sources[device_cols].astype(jnp.float32)
            partial_sum = jnp.einsum('trc,tcd->trd', device_values.astype(jnp.float32), picked)
            return jnp.einsum('tb,trd->brd', device_owners, partial_sum, precision=lax.Precision.HIGHEST)
        product = lax.map(device_product, (values, cols, owners))
        power_term = (product * inverse[:, :, :, None]).reshape(NODES, DIM)
        square_mean = lax.optimization_barrier(jnp.mean(power_term * power_term, axis=1))
        embedding = embedding + term_weights[level_index] * power_term * lax.rsqrt(square_mean + epsilon)[:, None]
        current = power_term.astype(jnp.bfloat16)
    return embedding
```

```python
import functools

import jax
import jax.numpy as jnp
from jax import lax
from jax.experimental import pallas as pl
from jax.experimental.pallas import tpu as pltpu
from jax.sharding import PartitionSpec as P

MESH = pl.DeviceIdType.MESH
DIM = 512
TERMS = 4
TILE = 128
BLOCKS = 4
SLOTS = 384
NY, NZ = 4, 8
NODES = NY * NZ
COLS = 8
HALVES = 2
WIDTH = DIM // COLS // HALVES
ROWS = BLOCKS * TILE
EPSILON = 1e-12
CHUNKS = 4

PLACE = (0, 1, 3, 5, 7, 6, 4, 2)
GROUPS = ((0, 12), (12, 8), (20, 8), (28, 4))


def slot_of(dy, dz):
    return PLACE[dz % NZ] * NY + dy % NY


OFFSETS = [
    (dy, dz) for dz in (4, 3, 5, 2, 6, 1, 7, 0) for dy in (2, 1, 3, 0) if (dy, dz) != (0, 0)
]


def group_of(slot):
    return [g for g, (first, count) in enumerate(GROUPS) if first <= slot < first + count][0]


def column(row):
    return jnp.transpose(jnp.broadcast_to(row, (TILE, TILE)))


def kernel(
    rows_ref, cols_ref, live_ref, degrees_ref, weights_ref, projection_hbm, values_hbm,
    out_ref,
    tiles, sums, matrix, gathered, staged, current, powers, squares, projected,
    meta_vmem, meta, wanted_vmem, wanted,
    tile_sem, local_sem, need_send, need_recv, send_sem, recv_sem, square_send, square_recv,
):
    node = lax.axis_index("node")
    col = lax.axis_index("col")
    y = node // NZ
    z = node - y * NZ

    def peer(dy, dz):
        return {"node": lax.rem(y + dy, NY) * NZ + lax.rem(z + dz, NZ), "col": col}

    def col_peer(d):
        return {"node": node, "col": lax.rem(col + d, COLS)}

    per = SLOTS // CHUNKS

    def load_tiles(i):
        part = pl.ds(i * per, per)
        return pltpu.make_async_copy(values_hbm.at[part], tiles.at[part], tile_sem.at[i])

    load_projection = pltpu.make_async_copy(projection_hbm, projected, local_sem.at[0])
    load_projection.start()
    for i in range(CHUNKS):
        load_tiles(i).start()

    barrier = pltpu.get_barrier_semaphore()
    for dy, dz in OFFSETS:
        pl.semaphore_signal(barrier, inc=1, device_id=peer(dy, dz), device_id_type=MESH)
    for d in range(1, COLS):
        pl.semaphore_signal(barrier, inc=1, device_id=col_peer(d), device_id_type=MESH)

    cols = cols_ref[...]
    token = lax.broadcasted_iota(jnp.int32, (3, TILE), 0) * TILE + lax.broadcasted_iota(
        jnp.int32, (3, TILE), 1
    )
    dy = ((cols >> 5) - y) & (NY - 1)
    dz = (((cols >> 2) & (NZ - 1)) - z) & (NZ - 1)
    place = jnp.where(dz <= NZ // 2, jnp.maximum(2 * dz - 1, 0), 2 * (NZ - dz))
    key = ((rows_ref[...] * NODES + place * NY + dy) * BLOCKS + (cols & (BLOCKS - 1))) * 512
    key = jnp.where(token < live_ref[0], key, TILE * BLOCKS * 512) + token
    lane = lax.broadcasted_iota(jnp.int32, (1, TILE), 1)
    tall = lax.broadcasted_iota(jnp.int32, (TILE, 1), 0)
    key_col = [column(key[c : c + 1]) for c in range(3)]
    rank = [
        sum(
            jnp.sum((key_col[b] < key[c : c + 1]).astype(jnp.int32), axis=0, keepdims=True)
            for b in range(3)
        )
        for c in range(3)
    ]
    rank_col = [column(rank[c]) for c in range(3)]
    pair_col = [k >> 11 for k in key_col]

    def pick(position, what):
        return sum(
            jnp.sum(jnp.where(rank_col[b] == position, what[b], 0), axis=0, keepdims=True)
            for b in range(3)
        )

    token_col = [jnp.broadcast_to(tall + b * TILE, (TILE, TILE)) for b in range(3)]
    for c in range(3):
        position = lane + c * TILE
        meta_vmem[c : c + 1] = pick(position, token_col)
        same = pick(position, pair_col) == pick(position - 1, pair_col)
        meta_vmem[3 + c : 4 + c] = (same & (position > 0)).astype(jnp.int32)
    upto = sum(jnp.sum((k <= lane).astype(jnp.int32), axis=0, keepdims=True) for k in pair_col)
    below = sum(jnp.sum((k < lane).astype(jnp.int32), axis=0, keepdims=True) for k in pair_col)
    meta_vmem[6:7] = jnp.maximum(upto - 1, 0)
    meta_vmem[7:8] = (upto > below).astype(jnp.int32)
    wanted_block = [
        jnp.where(
            (k < TILE * BLOCKS * 512) & (((k >> 11) & (NODES - 1)) == lane),
            (k >> 9) & (BLOCKS - 1),
            0,
        )
        for k in key_col
    ]
    need = functools.reduce(
        jnp.maximum, [jnp.max(w, axis=0, keepdims=True) for w in wanted_block]
    )
    wanted_vmem[0] = need
    load_meta = pltpu.make_async_copy(meta_vmem, meta, local_sem.at[1])
    load_meta.start()

    load_projection.wait()
    scaling = lax.rsqrt(jnp.maximum(degrees_ref[...], 1).astype(jnp.float32))
    for b in range(BLOCKS):
        block = projected[b * TILE : (b + 1) * TILE, :].astype(jnp.float32)
        block = jnp.transpose(block) * scaling[b : b + 1]
        for h in range(HALVES):
            current[h, b] = block[h * WIDTH : (h + 1) * WIDTH].astype(jnp.bfloat16)

    pl.semaphore_wait(barrier, len(OFFSETS) + COLS - 1)

    for dy, dz in OFFSETS:
        pltpu.make_async_remote_copy(
            src_ref=wanted_vmem.at[0],
            dst_ref=wanted_vmem.at[slot_of(-dy, -dz)],
            send_sem=need_send,
            recv_sem=need_recv,
            device_id=peer(dy, dz),
            device_id_type=MESH,
        ).start()

    for i in range(CHUNKS):
        load_tiles(i).wait()
    load_meta.wait()

    def add_tiles(c, acc):
        def add(i, acc):
            keep = meta[3 + c, i].astype(jnp.float32)
            acc = acc * keep + tiles[meta[c, i]].astype(jnp.float32)
            sums[c * TILE + i] = acc.astype(jnp.bfloat16)
            return acc

        return lax.fori_loop(0, TILE, add, acc, unroll=2)

    def need_copies():
        others = wanted_vmem.at[pl.ds(1, NODES - 1)]
        return pltpu.make_async_remote_copy(
            src_ref=others, dst_ref=others, send_sem=need_send, recv_sem=need_recv,
            device_id=peer(0, 1), device_id_type=MESH,
        )

    def send(k, h):
        for dy, dz in OFFSETS:
            to, at = slot_of(dy, dz), slot_of(-dy, -dz)
            staged[k, h, to] = current[h, wanted[to, 0, at]]
            pltpu.make_async_remote_copy(
                src_ref=staged.at[k, h, to],
                dst_ref=gathered.at[k, h, at],
                send_sem=send_sem.at[k, h],
                recv_sem=recv_sem.at[k, h, group_of(at)],
                device_id=peer(dy, dz),
                device_id_type=MESH,
            ).start()
        gathered[k, h, 0] = current[h, wanted[0, 0, 0]]

    def group_copies(k, h, first, count, g):
        part = gathered.at[k, h, pl.ds(first, count)]
        return pltpu.make_async_remote_copy(
            src_ref=part, dst_ref=part, send_sem=send_sem.at[k, h], recv_sem=recv_sem.at[k, h, g],
            device_id=peer(0, 1), device_id_type=MESH,
        )

    acc = add_tiles(0, jnp.zeros((TILE, TILE), jnp.float32))
    need_copies().wait_recv()
    load_wanted = pltpu.make_async_copy(wanted_vmem, wanted, local_sem.at[2])
    load_wanted.start()
    load_wanted.wait()
    for h in range(HALVES):
        send(0, h)
    acc = add_tiles(1, acc)
    acc = add_tiles(2, acc)

    def place_block(s, _):
        for r in range(BLOCKS):
            pair = r * NODES + s
            block = sums[meta[6, pair]] * meta[7, pair].astype(jnp.bfloat16)
            matrix[r * TILE : (r + 1) * TILE, pl.ds(pl.multiple_of(s * TILE, TILE), TILE)] = block
        return 0

    lax.fori_loop(0, NODES, place_block, 0)

    def times(x, first, count):
        part = matrix[:, first * TILE : (first + count) * TILE]
        return lax.dot_general(
            x, part, (((1,), (1,)), ((), ())), preferred_element_type=jnp.float32
        )

    ones = jnp.ones((16, TILE * 8), jnp.bfloat16)
    row_sum = sum(times(ones, first, 8) for first in range(0, NODES, 8))[0:1]
    inverse = 1.0 / jnp.maximum(row_sum, 1.0)

    def square_copies(k):
        others = squares.at[k, pl.ds(1, COLS - 1)]
        return pltpu.make_async_remote_copy(
            src_ref=others, dst_ref=others, send_sem=square_send.at[k],
            recv_sem=square_recv.at[k], device_id=col_peer(1), device_id_type=MESH,
        )

    for k in range(TERMS):
        square = jnp.zeros((1, ROWS), jnp.float32)
        for h in range(HALVES):
            power = jnp.zeros((WIDTH, ROWS), jnp.float32)
            for g, (first, count) in enumerate(GROUPS):
                skip = 1 if first == 0 else 0
                group_copies(k, h, first + skip, count - skip, g).wait_recv()
                x = jnp.concatenate([gathered[k, h, first + i] for i in range(count)], axis=1)
                power = power + times(x, first, count)
            power = power * inverse
            if k < TERMS - 1:
                for b in range(BLOCKS):
                    current[h, b] = power[:, b * TILE : (b + 1) * TILE].astype(jnp.bfloat16)
                send(k + 1, h)
            powers[k, h * WIDTH : (h + 1) * WIDTH] = power
            square = square + jnp.sum(power * power, axis=0, keepdims=True)
        squares[k, 0] = square
        for d in range(1, COLS):
            pltpu.make_async_remote_copy(
                src_ref=squares.at[k, 0],
                dst_ref=squares.at[k, COLS - d],
                send_sem=square_send.at[k],
                recv_sem=square_recv.at[k],
                device_id=col_peer(d),
                device_id_type=MESH,
            ).start()

    embedding = jnp.zeros((HALVES * WIDTH, ROWS), jnp.float32)
    for k in range(TERMS):
        square_copies(k).wait_recv()
        square = functools.reduce(jnp.add, [squares[k, d] for d in range(COLS)])
        factor = weights_ref[k] * lax.rsqrt(square * (1.0 / DIM) + EPSILON)
        embedding = embedding + powers[k] * factor
    out_ref[...] = embedding

    need_copies().wait_send()
    for k in range(TERMS):
        square_copies(k).wait_send()
        for h in range(HALVES):
            group_copies(k, h, 1, NODES - 1, 0).wait_send()


def local(tile_values, tile_rows, tile_cols, tile_live, degrees, projection, term_weights):
    vmem = pl.BlockSpec(memory_space=pltpu.VMEM)
    smem = pl.BlockSpec(memory_space=pltpu.SMEM)
    anywhere = pl.BlockSpec(memory_space=pl.ANY)
    width = HALVES * WIDTH
    bf16, f32, i32 = jnp.bfloat16, jnp.float32, jnp.int32
    out = pl.pallas_call(
        kernel,
        out_shape=jax.ShapeDtypeStruct((width, ROWS), f32),
        in_specs=[vmem, vmem, smem, vmem, smem, anywhere, anywhere],
        out_specs=vmem,
        scratch_shapes=[
            pltpu.VMEM((SLOTS, TILE, TILE), bf16),
            pltpu.VMEM((SLOTS, TILE, TILE), bf16),
            pltpu.VMEM((ROWS, NODES * TILE), bf16),
            pltpu.VMEM((TERMS, HALVES, NODES, WIDTH, TILE), bf16),
            pltpu.VMEM((TERMS, HALVES, NODES, WIDTH, TILE), bf16),
            pltpu.VMEM((HALVES, BLOCKS, WIDTH, TILE), bf16),
            pltpu.VMEM((TERMS, width, ROWS), f32),
            pltpu.VMEM((TERMS, COLS, 1, ROWS), f32),
            pltpu.VMEM((ROWS, width), i32),
            pltpu.VMEM((8, TILE), i32),
            pltpu.SMEM((8, TILE), i32),
            pltpu.VMEM((NODES, 1, TILE), i32),
            pltpu.SMEM((NODES, 1, TILE), i32),
            pltpu.SemaphoreType.DMA((CHUNKS,)),
            pltpu.SemaphoreType.DMA((3,)),
            pltpu.SemaphoreType.DMA,
            pltpu.SemaphoreType.DMA,
            pltpu.SemaphoreType.DMA((TERMS, HALVES)),
            pltpu.SemaphoreType.DMA((TERMS, HALVES, len(GROUPS))),
            pltpu.SemaphoreType.DMA((TERMS,)),
            pltpu.SemaphoreType.DMA((TERMS,)),
        ],
        compiler_params=pltpu.CompilerParams(
            collective_id=0, has_side_effects=True, vmem_limit_bytes=52 << 20
        ),
        cost_estimate=pl.CostEstimate(
            flops=2 * TERMS * width * ROWS * NODES * TILE,
            bytes_accessed=SLOTS * TILE * TILE * 2,
            transcendentals=0,
        ),
        name="embed",
    )(
        tile_rows.reshape(3, TILE),
        tile_cols.reshape(3, TILE),
        tile_live,
        degrees.reshape(BLOCKS, TILE),
        term_weights,
        projection,
        tile_values,
    )
    return out.T


def solution(mesh):
    placed = (
        P("node", None, None),
        P("node"),
        P("node"),
        P("node"),
        P("node"),
        P("node", "col"),
        P(),
    )
    return jax.shard_map(
        local, mesh=mesh, in_specs=placed, out_specs=P("node", "col"), check_vma=False
    )
```

```python
import functools

import jax
import jax.numpy as jnp
from jax import lax
from jax.experimental import pallas as pl
from jax.experimental.pallas import tpu as pltpu
from jax.sharding import PartitionSpec as P

MESH = pl.DeviceIdType.MESH
DIM = 512
TERMS = 4
TILE = 128
BLOCKS = 4
SLOTS = 384
NY, NZ = 4, 8
NODES = NY * NZ
COLS = 8
HALVES = 2
WIDTH = DIM // COLS // HALVES
ROWS = BLOCKS * TILE
EPSILON = 1e-12
CHUNKS = 4

PLACE = (0, 1, 3, 5, 7, 6, 4, 2)
GROUPS = ((0, 12), (12, 8), (20, 8), (28, 4))


def slot_of(dy, dz):
    return PLACE[dz % NZ] * NY + dy % NY


def turned(offset):
    return -offset[0], -offset[1]


DIRECT = [(dy, dz) for dz in (0, 1, -1) for dy in (2, 1, 3, 0) if (dy, dz) != (0, 0)]
HUBS = (2, -2)
READERS = {
    2: [(0, 2), (1, 2)] + [(dy, 1) for dy in (2, 1, 3, 0)] + [(2, 0), (1, 0), (3, 0)],
    -2: [(2, -2), (3, -2)] + [(dy, -1) for dy in (2, 1, 3, 0)] + [(2, 0), (1, 0), (3, 0)],
}
NEAR = [(dy, dz) for dz in (2, -2, 1, -1, 0) for dy in (2, 1, 3, 0) if (dy, dz) != (0, 0)]
KNOWN = len(NEAR) + 1
MESSAGES = len(DIRECT) + 2 * len(READERS[2])
ARRIVING = (11, 6, 8, 4)


def group_of(slot):
    return [g for g, (first, count) in enumerate(GROUPS) if first <= slot < first + count][0]


def column(row):
    return jnp.transpose(jnp.broadcast_to(row, (TILE, TILE)))


def kernel(
    rows_hbm, cols_hbm, live_ref, degrees_hbm, weights_ref, projection_hbm, values_hbm,
    out_ref,
    rows_ref, cols_ref, degrees_ref,
    tiles, sums, matrix, hub, held, relayed, gathered, staged, current, powers, squares, projected,
    meta_vmem, meta, wanted_vmem, wanted,
    tile_sem, local_sem, need_send, need_recv, hub_send, hub_recv, send_sem, recv_sem,
    square_send, square_recv,
):
    node = lax.axis_index("node")
    col = lax.axis_index("col")
    y = node // NZ
    z = node - y * NZ

    def peer(offset):
        dy, dz = offset
        return {"node": lax.rem(y + dy, NY) * NZ + lax.rem(z + dz + NZ, NZ), "col": col}

    def col_peer(d):
        return {"node": node, "col": lax.rem(col + d, COLS)}

    per = SLOTS // CHUNKS

    def load_tiles(i):
        part = pl.ds(i * per, per)
        return pltpu.make_async_copy(values_hbm.at[part], tiles.at[part], tile_sem.at[i])

    loads = [
        pltpu.make_async_copy(src, dst, local_sem.at[i])
        for i, (src, dst) in enumerate(
            [
                (cols_hbm, cols_ref),
                (rows_hbm, rows_ref),
                (degrees_hbm, degrees_ref),
                (projection_hbm, projected),
            ]
        )
    ]
    for load in loads:
        load.start()
    barrier = pltpu.get_barrier_semaphore()
    for offset in NEAR:
        pl.semaphore_signal(barrier, inc=1, device_id=peer(offset), device_id_type=MESH)
    for d in range(1, COLS):
        pl.semaphore_signal(barrier, inc=1, device_id=col_peer(d), device_id_type=MESH)
    for i in range(CHUNKS):
        load_tiles(i).start()
    for load in loads:
        load.wait()

    scaling = lax.rsqrt(jnp.maximum(degrees_ref[...], 1).astype(jnp.float32))
    for b in range(BLOCKS):
        block = projected[:, b * TILE : (b + 1) * TILE].astype(jnp.float32)
        block = block * scaling[b : b + 1]
        for h in range(HALVES):
            current[0, h, b] = block[h * WIDTH : (h + 1) * WIDTH].astype(jnp.bfloat16)

    cols = cols_ref[...]
    token = lax.broadcasted_iota(jnp.int32, (3, TILE), 0) * TILE + lax.broadcasted_iota(
        jnp.int32, (3, TILE), 1
    )
    dy = ((cols >> 5) - y) & (NY - 1)
    dz = (((cols >> 2) & (NZ - 1)) - z) & (NZ - 1)
    place = jnp.where(dz <= NZ // 2, jnp.maximum(2 * dz - 1, 0), 2 * (NZ - dz))
    key = ((rows_ref[...] * NODES + place * NY + dy) * BLOCKS + (cols & (BLOCKS - 1))) * 512
    key = jnp.where(token < live_ref[0], key, TILE * BLOCKS * 512) + token
    lane = lax.broadcasted_iota(jnp.int32, (1, TILE), 1)
    tall = lax.broadcasted_iota(jnp.int32, (TILE, 1), 0)
    key_col = [column(key[c : c + 1]) for c in range(3)]
    wanted_block = [
        jnp.where(
            (k < TILE * BLOCKS * 512) & (((k >> 11) & (NODES - 1)) == lane),
            (k >> 9) & (BLOCKS - 1),
            0,
        )
        for k in key_col
    ]
    wanted_vmem[0] = functools.reduce(
        jnp.maximum, [jnp.max(w, axis=0, keepdims=True) for w in wanted_block]
    )

    def need_copy(offset):
        return pltpu.make_async_remote_copy(
            src_ref=wanted_vmem.at[0],
            dst_ref=wanted_vmem.at[slot_of(*turned(offset))],
            send_sem=need_send,
            recv_sem=need_recv,
            device_id=peer(offset),
            device_id_type=MESH,
        )

    def need_copies():
        others = wanted_vmem.at[pl.ds(1, KNOWN - 1)]
        return pltpu.make_async_remote_copy(
            src_ref=others, dst_ref=others, send_sem=need_send, recv_sem=need_recv,
            device_id=peer((0, 1)), device_id_type=MESH,
        )

    def hub_copy(k, h, i):
        return pltpu.make_async_remote_copy(
            src_ref=current.at[k, h],
            dst_ref=hub.at[k, h, i],
            send_sem=hub_send.at[k, h, i],
            recv_sem=hub_recv.at[k, h, i],
            device_id=peer((0, HUBS[i])),
            device_id_type=MESH,
        )

    def send_hubs(k, h):
        for i in range(2):
            hub_copy(k, h, i).start()

    pl.semaphore_wait(barrier, len(NEAR) + COLS - 1)
    for h in range(HALVES):
        send_hubs(0, h)
    for offset in NEAR:
        need_copy(offset).start()

    rank = [
        sum(
            jnp.sum((key_col[b] < key[c : c + 1]).astype(jnp.int32), axis=0, keepdims=True)
            for b in range(3)
        )
        for c in range(3)
    ]
    rank_col = [column(rank[c]) for c in range(3)]
    pair_col = [k >> 11 for k in key_col]

    def pick(position, what):
        return sum(
            jnp.sum(jnp.where(rank_col[b] == position, what[b], 0), axis=0, keepdims=True)
            for b in range(3)
        )

    token_col = [jnp.broadcast_to(tall + b * TILE, (TILE, TILE)) for b in range(3)]
    for c in range(3):
        position = lane + c * TILE
        meta_vmem[c : c + 1] = pick(position, token_col)
        same = pick(position, pair_col) == pick(position - 1, pair_col)
        meta_vmem[3 + c : 4 + c] = (same & (position > 0)).astype(jnp.int32)
    upto = sum(jnp.sum((k <= lane).astype(jnp.int32), axis=0, keepdims=True) for k in pair_col)
    below = sum(jnp.sum((k < lane).astype(jnp.int32), axis=0, keepdims=True) for k in pair_col)
    meta_vmem[6:7] = jnp.maximum(upto - 1, 0)
    meta_vmem[7:8] = (upto > below).astype(jnp.int32)
    load_meta = pltpu.make_async_copy(meta_vmem, meta, local_sem.at[6])
    load_meta.start()
    for i in range(CHUNKS):
        load_tiles(i).wait()
    load_meta.wait()

    def add_tiles(c, acc):
        def add(i, acc):
            keep = meta[3 + c, i].astype(jnp.float32)
            acc = acc * keep + tiles[meta[c, i]].astype(jnp.float32)
            sums[c * TILE + i] = acc.astype(jnp.bfloat16)
            return acc

        return lax.fori_loop(0, TILE, add, acc, unroll=4)

    def send(k, h):
        for offset in DIRECT:
            to, at = slot_of(*offset), slot_of(*turned(offset))
            staged[k, h, to] = current[k, h, wanted[to, 0, at]]
        gathered[k, h, 0] = current[k, h, wanted[0, 0, 0]]
        for offset in DIRECT:
            to, at = slot_of(*offset), slot_of(*turned(offset))
            pltpu.make_async_remote_copy(
                src_ref=staged.at[k, h, to],
                dst_ref=gathered.at[k, h, at],
                send_sem=send_sem.at[k, h],
                recv_sem=recv_sem.at[k, h, group_of(at)],
                device_id=peer(offset),
                device_id_type=MESH,
            ).start()

    def relay(k, h):
        for i, d in enumerate(HUBS):
            hub_copy(k, h, i).wait_recv()
            held[i] = hub[k, h, i]
            places = [slot_of(-dy, -d - dz) for dy, dz in READERS[d]]
            for j, offset in enumerate(READERS[d]):
                relayed[k, h, i, j] = held[i, wanted[slot_of(*offset), 0, places[j]]]
            own = slot_of(0, -d)
            gathered[k, h, own] = held[i, wanted[0, 0, own]]
            for j, offset in enumerate(READERS[d]):
                pltpu.make_async_remote_copy(
                    src_ref=relayed.at[k, h, i, j],
                    dst_ref=gathered.at[k, h, places[j]],
                    send_sem=send_sem.at[k, h],
                    recv_sem=recv_sem.at[k, h, group_of(places[j])],
                    device_id=peer(offset),
                    device_id_type=MESH,
                ).start()

    def group_copies(k, h, count, g):
        part = gathered.at[k, h, pl.ds(0, count)]
        return pltpu.make_async_remote_copy(
            src_ref=part, dst_ref=part, send_sem=send_sem.at[k, h], recv_sem=recv_sem.at[k, h, g],
            device_id=peer((0, 1)), device_id_type=MESH,
        )

    acc = add_tiles(0, jnp.zeros((TILE, TILE), jnp.float32))
    need_copies().wait_recv()
    load_wanted = pltpu.make_async_copy(wanted_vmem, wanted, local_sem.at[7])
    load_wanted.start()
    load_wanted.wait()
    for h in range(HALVES):
        send(0, h)
    for h in range(HALVES):
        relay(0, h)
    acc = add_tiles(1, acc)
    acc = add_tiles(2, acc)

    def place_block(s, _):
        for r in range(BLOCKS):
            pair = r * NODES + s
            block = sums[meta[6, pair]] * meta[7, pair].astype(jnp.bfloat16)
            matrix[r * TILE : (r + 1) * TILE, pl.ds(pl.multiple_of(s * TILE, TILE), TILE)] = block
        return 0

    lax.fori_loop(0, NODES, place_block, 0)

    def times(x, first, count):
        part = matrix[:, first * TILE : (first + count) * TILE]
        return lax.dot_general(
            x, part, (((1,), (1,)), ((), ())), preferred_element_type=jnp.float32
        )

    def square_copies(k):
        others = squares.at[k, pl.ds(1, COLS - 1)]
        return pltpu.make_async_remote_copy(
            src_ref=others, dst_ref=others, send_sem=square_send.at[k],
            recv_sem=square_recv.at[k], device_id=col_peer(1), device_id_type=MESH,
        )

    def product(k, h):
        power = jnp.zeros((WIDTH + 16, ROWS), jnp.float32)
        for g, (first, count) in enumerate(GROUPS):
            group_copies(k, h, ARRIVING[g], g).wait_recv()
            x = jnp.concatenate([gathered[k, h, first + i] for i in range(count)], axis=1)
            x = jnp.concatenate([x, jnp.ones((16, count * TILE), jnp.bfloat16)], axis=0)
            power = power + times(x, first, count)
        power = power[:WIDTH] * (1.0 / jnp.maximum(power[WIDTH : WIDTH + 1], 1.0))
        powers[k, h * WIDTH : (h + 1) * WIDTH] = power
        return power

    def send_squares(k, parts):
        squares[k, 0] = sum(jnp.sum(p * p, axis=0, keepdims=True) for p in parts)
        for d in range(1, COLS):
            pltpu.make_async_remote_copy(
                src_ref=squares.at[k, 0],
                dst_ref=squares.at[k, COLS - d],
                send_sem=square_send.at[k],
                recv_sem=square_recv.at[k],
                device_id=col_peer(d),
                device_id_type=MESH,
            ).start()

    for k in range(TERMS):
        parts = []
        for h in range(HALVES):
            power = product(k, h)
            parts.append(power)
            if k < TERMS - 1:
                for b in range(BLOCKS):
                    part = power[:, b * TILE : (b + 1) * TILE]
                    current[k + 1, h, b] = part.astype(jnp.bfloat16)
                send_hubs(k + 1, h)
                send(k + 1, h)
        if k < TERMS - 1:
            for h in range(HALVES):
                relay(k + 1, h)
        send_squares(k, parts)

    embedding = jnp.zeros((HALVES * WIDTH, ROWS), jnp.float32)
    for k in range(TERMS):
        square_copies(k).wait_recv()
        square = functools.reduce(jnp.add, [squares[k, d] for d in range(COLS)])
        factor = weights_ref[k] * lax.rsqrt(square * (1.0 / DIM) + EPSILON)
        embedding = embedding + powers[k] * factor
    out_ref[...] = embedding

    need_copies().wait_send()
    for k in range(TERMS):
        square_copies(k).wait_send()
        for h in range(HALVES):
            group_copies(k, h, MESSAGES, 0).wait_send()
            for i in range(2):
                hub_copy(k, h, i).wait_send()


def local(tile_values, tile_rows, tile_cols, tile_live, degrees, projection, term_weights):
    vmem = pl.BlockSpec(memory_space=pltpu.VMEM)
    smem = pl.BlockSpec(memory_space=pltpu.SMEM)
    anywhere = pl.BlockSpec(memory_space=pl.ANY)
    width = HALVES * WIDTH
    bf16, f32, i32 = jnp.bfloat16, jnp.float32, jnp.int32
    out = pl.pallas_call(
        kernel,
        out_shape=jax.ShapeDtypeStruct((width, ROWS), f32),
        in_specs=[anywhere, anywhere, smem, anywhere, smem, anywhere, anywhere],
        out_specs=vmem,
        scratch_shapes=[
            pltpu.VMEM((3, TILE), i32),
            pltpu.VMEM((3, TILE), i32),
            pltpu.VMEM((BLOCKS, TILE), i32),
            pltpu.VMEM((SLOTS, TILE, TILE), bf16),
            pltpu.VMEM((SLOTS, TILE, TILE), bf16),
            pltpu.VMEM((ROWS, NODES * TILE), bf16),
            pltpu.VMEM((TERMS, HALVES, 2, BLOCKS, WIDTH, TILE), bf16),
            pltpu.VMEM((2, BLOCKS, WIDTH, TILE), bf16),
            pltpu.VMEM((TERMS, HALVES, 2, len(READERS[2]), WIDTH, TILE), bf16),
            pltpu.VMEM((TERMS, HALVES, NODES, WIDTH, TILE), bf16),
            pltpu.VMEM((TERMS, HALVES, len(DIRECT) + 1, WIDTH, TILE), bf16),
            pltpu.VMEM((TERMS, HALVES, BLOCKS, WIDTH, TILE), bf16),
            pltpu.VMEM((TERMS, width, ROWS), f32),
            pltpu.VMEM((TERMS, COLS, 1, ROWS), f32),
            pltpu.VMEM((width, ROWS), i32),
            pltpu.VMEM((8, TILE), i32),
            pltpu.SMEM((8, TILE), i32),
            pltpu.VMEM((KNOWN, 1, TILE), i32),
            pltpu.SMEM((KNOWN, 1, TILE), i32),
            pltpu.SemaphoreType.DMA((CHUNKS,)),
            pltpu.SemaphoreType.DMA((8,)),
            pltpu.SemaphoreType.DMA,
            pltpu.SemaphoreType.DMA,
            pltpu.SemaphoreType.DMA((TERMS, HALVES, 2)),
            pltpu.SemaphoreType.DMA((TERMS, HALVES, 2)),
            pltpu.SemaphoreType.DMA((TERMS, HALVES)),
            pltpu.SemaphoreType.DMA((TERMS, HALVES, len(GROUPS))),
            pltpu.SemaphoreType.DMA((TERMS,)),
            pltpu.SemaphoreType.DMA((TERMS,)),
        ],
        compiler_params=pltpu.CompilerParams(
            collective_id=0, has_side_effects=True, vmem_limit_bytes=60 << 20
        ),
        cost_estimate=pl.CostEstimate(
            flops=2 * TERMS * width * ROWS * NODES * TILE,
            bytes_accessed=SLOTS * TILE * TILE * 2,
            transcendentals=0,
        ),
        name="embed",
    )(
        tile_rows.reshape(3, TILE),
        tile_cols.reshape(3, TILE),
        tile_live,
        degrees.reshape(BLOCKS, TILE),
        term_weights,
        projection.T,
        tile_values,
    )
    return out.T


def solution(mesh):
    placed = (
        P("node", None, None),
        P("node"),
        P("node"),
        P("node"),
        P("node"),
        P("node", "col"),
        P(),
    )
    return jax.shard_map(
        local, mesh=mesh, in_specs=placed, out_specs=P("node", "col"), check_vma=False
    )
```

```python
import functools

import jax
import jax.numpy as jnp
from jax import lax
from jax.experimental import pallas as pl
from jax.experimental.pallas import tpu as pltpu
from jax.sharding import PartitionSpec as P

MESH = pl.DeviceIdType.MESH
DIM = 512
TERMS = 4
TILE = 128
BLOCKS = 4
SLOTS = 384
NY, NZ = 4, 8
NODES = NY * NZ
COLS = 8
HALVES = 2
WIDTH = DIM // COLS // HALVES
ROWS = BLOCKS * TILE
EPSILON = 1e-12
CHUNKS = 4

PLACE = (0, 1, 3, 5, 7, 6, 4, 2)
GROUPS = ((0, 12), (12, 8), (20, 8), (28, 4))


def slot_of(dy, dz):
    return PLACE[dz % NZ] * NY + dy % NY


def turned(offset):
    return -offset[0], -offset[1]


DIRECT = [(dy, dz) for dz in (0, 1, -1) for dy in (2, 1, 3, 0) if (dy, dz) != (0, 0)]
HUBS = (2, -2)
READERS = {
    2: [(0, 2), (1, 2)] + [(dy, 1) for dy in (2, 1, 3, 0)] + [(2, 0), (1, 0), (3, 0)],
    -2: [(2, -2), (3, -2)] + [(dy, -1) for dy in (2, 1, 3, 0)] + [(2, 0), (1, 0), (3, 0)],
}
NEAR = [(dy, dz) for dz in (2, -2, 1, -1, 0) for dy in (2, 1, 3, 0) if (dy, dz) != (0, 0)]
KNOWN = len(NEAR) + 1
MESSAGES = len(DIRECT) + 2 * len(READERS[2])
ARRIVING = (11, 6, 8, 4)


def group_of(slot):
    return [g for g, (first, count) in enumerate(GROUPS) if first <= slot < first + count][0]


def column(row):
    return jnp.transpose(jnp.broadcast_to(row, (TILE, TILE)))


def kernel(
    rows_hbm, cols_hbm, live_ref, degrees_hbm, weights_ref, projection_hbm, values_hbm,
    out_ref,
    rows_ref, cols_ref, degrees_ref,
    tiles, sums, matrix, hub, held, relayed, gathered, staged, current, powers, squares, projected,
    meta_vmem, meta, wanted_vmem, wanted,
    tile_sem, local_sem, need_send, need_recv, hub_send, hub_recv, send_sem, recv_sem,
    square_send, square_recv,
):
    node = lax.axis_index("node")
    col = lax.axis_index("col")
    y = node // NZ
    z = node - y * NZ

    def peer(offset):
        dy, dz = offset
        return {"node": lax.rem(y + dy, NY) * NZ + lax.rem(z + dz + NZ, NZ), "col": col}

    def col_peer(d):
        return {"node": node, "col": lax.rem(col + d, COLS)}

    per = SLOTS // CHUNKS

    def load_tiles(i):
        part = pl.ds(i * per, per)
        return pltpu.make_async_copy(values_hbm.at[part], tiles.at[part], tile_sem.at[i])

    loads = [
        pltpu.make_async_copy(src, dst, local_sem.at[i])
        for i, (src, dst) in enumerate(
            [
                (cols_hbm, cols_ref),
                (rows_hbm, rows_ref),
                (degrees_hbm, degrees_ref),
                (projection_hbm, projected),
            ]
        )
    ]
    for load in loads:
        load.start()
    barrier = pltpu.get_barrier_semaphore()
    for offset in NEAR:
        pl.semaphore_signal(barrier, inc=1, device_id=peer(offset), device_id_type=MESH)
    for d in range(1, COLS):
        pl.semaphore_signal(barrier, inc=1, device_id=col_peer(d), device_id_type=MESH)
    for i in range(CHUNKS):
        load_tiles(i).start()
    for load in loads:
        load.wait()

    scaling = lax.rsqrt(jnp.maximum(degrees_ref[...], 1).astype(jnp.float32))
    for b in range(BLOCKS):
        block = projected[:, b * TILE : (b + 1) * TILE].astype(jnp.float32)
        block = block * scaling[b : b + 1]
        for h in range(HALVES):
            current[0, h, b] = block[h * WIDTH : (h + 1) * WIDTH].astype(jnp.bfloat16)

    cols = cols_ref[...]
    token = lax.broadcasted_iota(jnp.int32, (3, TILE), 0) * TILE + lax.broadcasted_iota(
        jnp.int32, (3, TILE), 1
    )
    dy = ((cols >> 5) - y) & (NY - 1)
    dz = (((cols >> 2) & (NZ - 1)) - z) & (NZ - 1)
    place = jnp.where(dz <= NZ // 2, jnp.maximum(2 * dz - 1, 0), 2 * (NZ - dz))
    key = ((rows_ref[...] * NODES + place * NY + dy) * BLOCKS + (cols & (BLOCKS - 1))) * 512
    key = jnp.where(token < live_ref[0], key, TILE * BLOCKS * 512) + token
    lane = lax.broadcasted_iota(jnp.int32, (1, TILE), 1)
    tall = lax.broadcasted_iota(jnp.int32, (TILE, 1), 0)
    key_col = [column(key[c : c + 1]) for c in range(3)]
    wanted_block = [
        jnp.where(
            (k < TILE * BLOCKS * 512) & (((k >> 11) & (NODES - 1)) == lane),
            (k >> 9) & (BLOCKS - 1),
            0,
        )
        for k in key_col
    ]
    wanted_vmem[0] = functools.reduce(
        jnp.maximum, [jnp.max(w, axis=0, keepdims=True) for w in wanted_block]
    )

    def need_copy(offset):
        return pltpu.make_async_remote_copy(
            src_ref=wanted_vmem.at[0],
            dst_ref=wanted_vmem.at[slot_of(*turned(offset))],
            send_sem=need_send,
            recv_sem=need_recv,
            device_id=peer(offset),
            device_id_type=MESH,
        )

    def need_copies():
        others = wanted_vmem.at[pl.ds(1, KNOWN - 1)]
        return pltpu.make_async_remote_copy(
            src_ref=others, dst_ref=others, send_sem=need_send, recv_sem=need_recv,
            device_id=peer((0, 1)), device_id_type=MESH,
        )

    def hub_copy(k, h, i):
        return pltpu.make_async_remote_copy(
            src_ref=current.at[k, h],
            dst_ref=hub.at[k, h, i],
            send_sem=hub_send.at[k, h, i],
            recv_sem=hub_recv.at[k, h, i],
            device_id=peer((0, HUBS[i])),
            device_id_type=MESH,
        )

    def send_hubs(k, h):
        for i in range(2):
            hub_copy(k, h, i).start()

    pl.semaphore_wait(barrier, len(NEAR) + COLS - 1)
    for h in range(HALVES):
        send_hubs(0, h)
    for offset in NEAR:
        need_copy(offset).start()

    rank = [
        sum(
            jnp.sum((key_col[b] < key[c : c + 1]).astype(jnp.int32), axis=0, keepdims=True)
            for b in range(3)
        )
        for c in range(3)
    ]
    rank_col = [column(rank[c]) for c in range(3)]
    pair_col = [k >> 11 for k in key_col]

    def pick(position, what):
        return sum(
            jnp.sum(jnp.where(rank_col[b] == position, what[b], 0), axis=0, keepdims=True)
            for b in range(3)
        )

    token_col = [jnp.broadcast_to(tall + b * TILE, (TILE, TILE)) for b in range(3)]
    for c in range(3):
        position = lane + c * TILE
        meta_vmem[c : c + 1] = pick(position, token_col)
        same = pick(position, pair_col) == pick(position - 1, pair_col)
        meta_vmem[3 + c : 4 + c] = (same & (position > 0)).astype(jnp.int32)
    upto = sum(jnp.sum((k <= lane).astype(jnp.int32), axis=0, keepdims=True) for k in pair_col)
    below = sum(jnp.sum((k < lane).astype(jnp.int32), axis=0, keepdims=True) for k in pair_col)
    meta_vmem[6:7] = jnp.maximum(upto - 1, 0)
    meta_vmem[7:8] = (upto > below).astype(jnp.int32)
    load_meta = pltpu.make_async_copy(meta_vmem, meta, local_sem.at[6])
    load_meta.start()
    for i in range(CHUNKS):
        load_tiles(i).wait()
    load_meta.wait()

    def add_tiles(c, acc):
        def add(i, acc):
            keep = meta[3 + c, i].astype(jnp.float32)
            acc = acc * keep + tiles[meta[c, i]].astype(jnp.float32)
            sums[c * TILE + i] = acc.astype(jnp.bfloat16)
            return acc

        return lax.fori_loop(0, TILE, add, acc, unroll=4)

    def send(k, h):
        for offset in DIRECT:
            to, at = slot_of(*offset), slot_of(*turned(offset))
            staged[k, h, to] = current[k, h, wanted[to, 0, at]]
        gathered[k, h, 0] = current[k, h, wanted[0, 0, 0]]
        for offset in DIRECT:
            to, at = slot_of(*offset), slot_of(*turned(offset))
            pltpu.make_async_remote_copy(
                src_ref=staged.at[k, h, to],
                dst_ref=gathered.at[k, h, at],
                send_sem=send_sem.at[k, h],
                recv_sem=recv_sem.at[k, h, group_of(at)],
                device_id=peer(offset),
                device_id_type=MESH,
            ).start()

    def relay(k, h):
        for i, d in enumerate(HUBS):
            hub_copy(k, h, i).wait_recv()
            held[i] = hub[k, h, i]
            places = [slot_of(-dy, -d - dz) for dy, dz in READERS[d]]
            for j, offset in enumerate(READERS[d]):
                relayed[k, h, i, j] = held[i, wanted[slot_of(*offset), 0, places[j]]]
            own = slot_of(0, -d)
            gathered[k, h, own] = held[i, wanted[0, 0, own]]
            for j, offset in enumerate(READERS[d]):
                pltpu.make_async_remote_copy(
                    src_ref=relayed.at[k, h, i, j],
                    dst_ref=gathered.at[k, h, places[j]],
                    send_sem=send_sem.at[k, h],
                    recv_sem=recv_sem.at[k, h, group_of(places[j])],
                    device_id=peer(offset),
                    device_id_type=MESH,
                ).start()

    def group_copies(k, h, count, g):
        part = gathered.at[k, h, pl.ds(0, count)]
        return pltpu.make_async_remote_copy(
            src_ref=part, dst_ref=part, send_sem=send_sem.at[k, h], recv_sem=recv_sem.at[k, h, g],
            device_id=peer((0, 1)), device_id_type=MESH,
        )

    acc = add_tiles(0, jnp.zeros((TILE, TILE), jnp.float32))
    need_copies().wait_recv()
    load_wanted = pltpu.make_async_copy(wanted_vmem, wanted, local_sem.at[7])
    load_wanted.start()
    load_wanted.wait()
    for h in range(HALVES):
        send(0, h)
    for h in range(HALVES):
        relay(0, h)
    acc = add_tiles(1, acc)
    acc = add_tiles(2, acc)

    def place_block(s, _):
        for r in range(BLOCKS):
            pair = r * NODES + s
            block = sums[meta[6, pair]] * meta[7, pair].astype(jnp.bfloat16)
            matrix[pl.ds(pl.multiple_of(s * TILE, TILE), TILE), r * TILE : (r + 1) * TILE] = jnp.transpose(block)
        return 0

    lax.fori_loop(0, NODES, place_block, 0)

    def times(x, first, count):
        part = matrix[first * TILE : (first + count) * TILE, :]
        return lax.dot_general(
            x, part, (((1,), (0,)), ((), ())), preferred_element_type=jnp.float32
        )

    def square_copies(k):
        others = squares.at[k, pl.ds(1, COLS - 1)]
        return pltpu.make_async_remote_copy(
            src_ref=others, dst_ref=others, send_sem=square_send.at[k],
            recv_sem=square_recv.at[k], device_id=col_peer(1), device_id_type=MESH,
        )

    def product(k, h):
        power = jnp.zeros((WIDTH + 16, ROWS), jnp.float32)
        for g, (first, count) in enumerate(GROUPS):
            group_copies(k, h, ARRIVING[g], g).wait_recv()
            x = jnp.concatenate([gathered[k, h, first + i] for i in range(count)], axis=1)
            x = jnp.concatenate([x, jnp.ones((16, count * TILE), jnp.bfloat16)], axis=0)
            power = power + times(x, first, count)
        power = power[:WIDTH] * (1.0 / jnp.maximum(power[WIDTH : WIDTH + 1], 1.0))
        powers[k, h * WIDTH : (h + 1) * WIDTH] = power
        return power

    def send_squares(k, parts):
        squares[k, 0] = sum(jnp.sum(p * p, axis=0, keepdims=True) for p in parts)
        for d in range(1, COLS):
            pltpu.make_async_remote_copy(
                src_ref=squares.at[k, 0],
                dst_ref=squares.at[k, COLS - d],
                send_sem=square_send.at[k],
                recv_sem=square_recv.at[k],
                device_id=col_peer(d),
                device_id_type=MESH,
            ).start()

    for k in range(TERMS):
        parts = []
        for h in range(HALVES):
            power = product(k, h)
            parts.append(power)
            if k < TERMS - 1:
                for b in range(BLOCKS):
                    part = power[:, b * TILE : (b + 1) * TILE]
                    current[k + 1, h, b] = part.astype(jnp.bfloat16)
                send_hubs(k + 1, h)
                send(k + 1, h)
        if k < TERMS - 1:
            for h in range(HALVES):
                relay(k + 1, h)
        send_squares(k, parts)

    embedding = jnp.zeros((HALVES * WIDTH, ROWS), jnp.float32)
    for k in range(TERMS):
        square_copies(k).wait_recv()
        square = functools.reduce(jnp.add, [squares[k, d] for d in range(COLS)])
        factor = weights_ref[k] * lax.rsqrt(square * (1.0 / DIM) + EPSILON)
        embedding = embedding + powers[k] * factor
    out_ref[...] = embedding

    need_copies().wait_send()
    for k in range(TERMS):
        square_copies(k).wait_send()
        for h in range(HALVES):
            group_copies(k, h, MESSAGES, 0).wait_send()
            for i in range(2):
                hub_copy(k, h, i).wait_send()


def local(tile_values, tile_rows, tile_cols, tile_live, degrees, projection, term_weights):
    vmem = pl.BlockSpec(memory_space=pltpu.VMEM)
    smem = pl.BlockSpec(memory_space=pltpu.SMEM)
    anywhere = pl.BlockSpec(memory_space=pl.ANY)
    width = HALVES * WIDTH
    bf16, f32, i32 = jnp.bfloat16, jnp.float32, jnp.int32
    out = pl.pallas_call(
        kernel,
        out_shape=jax.ShapeDtypeStruct((width, ROWS), f32),
        in_specs=[anywhere, anywhere, smem, anywhere, smem, anywhere, anywhere],
        out_specs=vmem,
        scratch_shapes=[
            pltpu.VMEM((3, TILE), i32),
            pltpu.VMEM((3, TILE), i32),
            pltpu.VMEM((BLOCKS, TILE), i32),
            pltpu.VMEM((SLOTS, TILE, TILE), bf16),
            pltpu.VMEM((SLOTS, TILE, TILE), bf16),
            pltpu.VMEM((NODES * TILE, ROWS), bf16),
            pltpu.VMEM((TERMS, HALVES, 2, BLOCKS, WIDTH, TILE), bf16),
            pltpu.VMEM((2, BLOCKS, WIDTH, TILE), bf16),
            pltpu.VMEM((TERMS, HALVES, 2, len(READERS[2]), WIDTH, TILE), bf16),
            pltpu.VMEM((TERMS, HALVES, NODES, WIDTH, TILE), bf16),
            pltpu.VMEM((TERMS, HALVES, len(DIRECT) + 1, WIDTH, TILE), bf16),
            pltpu.VMEM((TERMS, HALVES, BLOCKS, WIDTH, TILE), bf16),
            pltpu.VMEM((TERMS, width, ROWS), f32),
            pltpu.VMEM((TERMS, COLS, 1, ROWS), f32),
            pltpu.VMEM((width, ROWS), i32),
            pltpu.VMEM((8, TILE), i32),
            pltpu.SMEM((8, TILE), i32),
            pltpu.VMEM((KNOWN, 1, TILE), i32),
            pltpu.SMEM((KNOWN, 1, TILE), i32),
            pltpu.SemaphoreType.DMA((CHUNKS,)),
            pltpu.SemaphoreType.DMA((8,)),
            pltpu.SemaphoreType.DMA,
            pltpu.SemaphoreType.DMA,
            pltpu.SemaphoreType.DMA((TERMS, HALVES, 2)),
            pltpu.SemaphoreType.DMA((TERMS, HALVES, 2)),
            pltpu.SemaphoreType.DMA((TERMS, HALVES)),
            pltpu.SemaphoreType.DMA((TERMS, HALVES, len(GROUPS))),
            pltpu.SemaphoreType.DMA((TERMS,)),
            pltpu.SemaphoreType.DMA((TERMS,)),
        ],
        compiler_params=pltpu.CompilerParams(
            collective_id=0, has_side_effects=True, vmem_limit_bytes=60 << 20
        ),
        cost_estimate=pl.CostEstimate(
            flops=2 * TERMS * width * ROWS * NODES * TILE,
            bytes_accessed=SLOTS * TILE * TILE * 2,
            transcendentals=0,
        ),
        name="embed",
    )(
        tile_rows.reshape(3, TILE),
        tile_cols.reshape(3, TILE),
        tile_live,
        degrees.reshape(BLOCKS, TILE),
        term_weights,
        projection.T,
        tile_values,
    )
    return out.T


def solution(mesh):
    placed = (
        P("node", None, None),
        P("node"),
        P("node"),
        P("node"),
        P("node"),
        P("node", "col"),
        P(),
    )
    return jax.shard_map(
        local, mesh=mesh, in_specs=placed, out_specs=P("node", "col"), check_vma=False
    )
```
